512 devices in a mesh: band: 32 (over y, x), field: 16 (over z, core).
Axes of the slice: x: 4, y: 8, z: 8, core: 2. Of those that a mesh axis runs over, the one named last changes fastest.
Arguments:
- fourier: bfloat16 [144, 1024, 2, 1024], P('field', 'band'), may hold values from -6 to 6
- row_length: int32 [1024], P('band'), may hold values from 20 to 2076, as said below
- wave_order: int32 [512], replicated, may hold values from 0 to 511, each once
- legendre: bfloat16 [512, 1025, 512], P(('band', 'field')), may hold values from -0.1875 to 0.1875
- vertical: bfloat16 [2, 72, 72], replicated, may hold values from -0.75 to 0.75
Outputs:
- returned: bfloat16 [144, 1024, 2, 1024], P('field', 'band')
The draws below stay inside these ranges and needn't reach their ends.
Inputs may be any that keep to these rules, and one draw needn't show every extreme that they name: row_length[lat] is a multiple of 4 lying 0 to 12 above 20 + 4 * d with d = min(lat, 1023 - lat); the two polar rows have length 20 and the two rows beside the equator lie 12 above. `wave_order`: each pair index appears once.
All inputs are finite; a program needn't handle non-finite values.
Results may differ from the reference program's by a relative error of at most 0.0049.
Values may be sent and summed in bfloat16 or wider, within the bound.
No kernel may reach another device: no remote copies, remote signals or barrier semaphores. Data moves between devices by JAX's collectives and lax.ppermute only.
A program may use at most 64 MiB of HBM per device.

```python
import jax
import jax.numpy as jnp
from jax import lax

MW = 1024
LEV = 72
NLAT = 1024
NLATH = 512
FL = 144
NPAIR = 512
ROW_STEP = 4


def draw_row_length(key, part):
    lat_ids = jnp.arange(NLAT, dtype=jnp.int32)
    from_pole = jnp.minimum(lat_ids, NLAT - 1 - lat_ids)
    jitter = jax.random.randint(key, (NLAT,), 0, 4, dtype=jnp.int32)
    jitter = jnp.where(from_pole == 0, 0, jitter)
    jitter = jnp.where(from_pole == NLAT // 2 - 1, 3, jitter)
    return (20 + ROW_STEP * from_pole + 4 * jitter).astype(jnp.int32)


def steps_of(stream_key, extent, split, low, top_value):
    gain, own = 1.0, jax.random.fold_in(stream_key, 6)
    for dim, blocks in split:
        heights = jnp.exp(jax.random.uniform(jax.random.fold_in(own, dim), (blocks,), jnp.float32, low / len(split), top_value / len(split)))
        gain = gain * jnp.repeat(heights, extent[dim] // blocks).reshape([-1 if axis == dim else 1 for axis in range(len(extent))])
    return gain


def bell_draw(stream_key, dims, deviation, limit, cuts=(), kind=jnp.bfloat16):
    level = steps_of(stream_key, dims, cuts, -0.22, 0.18) if cuts else 1.0
    result = jax.random.normal(stream_key, dims, jnp.float32) * deviation * level
    return jnp.minimum(jnp.maximum(result, -limit), limit).astype(kind)


def setup_inputs(seed: int = 0) -> dict:
    splits = jax.random.split(jax.random.key(seed), 6)
    fourier = bell_draw(splits[0], (FL, NLAT, 2, MW), 1.0, 6.0, ((0, 16), (1, 32)))
    row_length = draw_row_length(jax.random.fold_in(splits[5], 71), 0)
    wave_order = jax.random.permutation(splits[2], NPAIR).astype(jnp.int32)
    legendre = bell_draw(splits[3], (NPAIR, MW + 1, NLATH), NLAT ** -0.5, 0.1875, ((0, 512),))
    vertical = bell_draw(splits[4], (2, LEV, LEV), LEV ** -0.5, 0.75)
    return {"fourier": fourier, "row_length": row_length, "wave_order": wave_order, "legendre": legendre, "vertical": vertical}


def pair_table(table_pair, first_wave):
    row_ids = jnp.arange(MW + 1, dtype=jnp.int32)
    boundary = MW - first_wave
    degree = jnp.where(row_ids < boundary, row_ids, row_ids - boundary)
    parity = (1 - 2 * (degree % 2)).astype(jnp.float32)
    northern = table_pair.astype(jnp.float32)
    southern = jnp.flip(northern, axis=1) * parity[:, None]
    owner_mask = jnp.stack([row_ids < boundary, row_ids >= boundary])
    return jnp.concatenate([northern, southern], axis=1), owner_mask


def reference(fourier, row_length, wave_order, legendre, vertical):
    wave_ids = jnp.arange(MW, dtype=jnp.int32)
    wave_count = jnp.minimum(MW, row_length // 2)
    in_range = wave_ids[None, :] < wave_count[:, None]
    masked = jnp.where(in_range[None, :, None, :], fourier, jnp.zeros((), fourier.dtype))
    ordering = jnp.stack([wave_order, MW - 1 - wave_order], axis=1).reshape(MW)
    paired = jnp.take(masked, ordering, axis=3).reshape(FL, NLAT, 2, NPAIR, 2).transpose(3, 4, 0, 2, 1)
    mixing = vertical.astype(jnp.float32)
    highest = lax.Precision.HIGHEST

    def transform_pair(inputs):
        values, table_pair, first_wave = inputs
        full_table, owner_mask = pair_table(table_pair, first_wave)
        flat_values = values.reshape(2, FL * 2, NLAT).astype(jnp.float32)
        spectral = jnp.einsum("scl,rl->scr", flat_values, full_table, precision=highest)
        spectral = jnp.where(owner_mask[:, None, :], spectral, 0.0).astype(jnp.bfloat16)
        shaped = spectral.reshape(2, 2, LEV, 2, MW + 1).astype(jnp.float32)
        updated = jnp.einsum("qab,sqbcr->sqacr", mixing, shaped, precision=highest).astype(jnp.bfloat16)
        updated_flat = updated.reshape(2, FL * 2, MW + 1).astype(jnp.float32)
        grid_part = jnp.einsum("scr,rl->scl", updated_flat, full_table, precision=highest)
        return grid_part.astype(jnp.bfloat16).reshape(2, FL, 2, NLAT)

    pieces = lax.map(transform_pair, (paired, legendre, wave_order))
    sorted_back = pieces.transpose(2, 4, 3, 0, 1).reshape(FL, NLAT, 2, MW)
    position = jnp.zeros((MW,), jnp.int32).at[ordering].set(wave_ids)
    restored = jnp.take(sorted_back, position, axis=3)
    return jnp.where(in_range[None, :, None, :], restored, jnp.zeros((), restored.dtype))
```

```python
import functools

import jax
import jax.numpy as jnp
from jax import lax
from jax.experimental import pallas as pl
from jax.experimental.pallas import tpu as pltpu
from jax.sharding import PartitionSpec as P

BF16 = jnp.bfloat16
F32 = jnp.float32
ROWS = 1152
NT = (((1,), (1,)), ((), ()))
NN = (((1,), (0,)), ((), ()))


def dot(a, b, dims=NN):
    return lax.dot_general(a, b, dims, preferred_element_type=F32)


def pair_kernel(
    boundary_ref, data_ref, table_ref, mix_ref, north_ref, south_ref, out_ref,
    value_n, value_s, spectral, updated, flipped, grid_n, grid_s,
):
    halves = ((north_ref, value_n, grid_n, 0), (south_ref, value_s, grid_s, 1))

    def source(tile, half, part, width):
        rows = []
        for high in range(4):
            start = ((half * 4 + high) * 4 + part) * 32
            rows.append(data_ref[start : start + 32, tile * 128 : tile * 128 + width])
        return jnp.concatenate(rows, axis=0)

    for tile in range(5):
        width = 128 if tile < 4 else 64
        groups = width // 32
        for perm_ref, value_ref, _, half in halves:
            moved = jnp.zeros((128, groups * 128), F32)
            if width == 128:
                joined = jnp.concatenate(
                    [source(tile, half, part, width) for part in range(4)], axis=1
                )
                moved = dot(joined, perm_ref[...])
            else:
                for part in range(4):
                    moved += dot(
                        source(tile, half, part, width),
                        perm_ref[part * 128 : part * 128 + width, : groups * 128],
                    )
            moved = moved.astype(BF16)
            for high in range(4):
                place = high if half == 0 else 3 - high
                for group in range(groups):
                    row = (tile * 4 + group) * 32
                    value_ref[row : row + 32, place * 128 : place * 128 + 128] = moved[
                        high * 32 : high * 32 + 32, group * 128 : group * 128 + 128
                    ]

    boundary = boundary_ref[0]
    for start in range(0, ROWS, 256):
        size = min(256, ROWS - start)
        row_ids = lax.broadcasted_iota(jnp.int32, (1, size), 1) + start
        first = row_ids < boundary
        degree = jnp.where(first, row_ids, row_ids - boundary)
        parity = (1 - 2 * (degree & 1)).astype(F32)
        slots = lax.broadcasted_iota(jnp.int32, (576, size), 0) & 1
        owned = slots == jnp.where(first, 0, 1)
        table = table_ref[start : start + size, :]
        total = dot(value_n[...], table, NT) + parity * dot(value_s[...], table, NT)
        spectral[...] = jnp.zeros_like(spectral)
        spectral[:, :size] = jnp.where(owned, total, 0.0).astype(BF16)
        mixed = dot(mix_ref[...], spectral[:, :size])
        updated[:, start : start + size] = mixed.astype(BF16)
        flipped[:, start : start + size] = (mixed * parity).astype(BF16)

    grid_n[...] = dot(updated[...], table_ref[...]).astype(BF16)
    grid_s[...] = dot(flipped[...], table_ref[...]).astype(BF16)

    for tile in range(5):
        width = 128 if tile < 4 else 64
        groups = width // 32
        for perm_ref, _, grid_ref, half in halves:
            lanes = []
            for group in range(groups):
                row = (tile * 4 + group) * 32
                rows = []
                for high in range(4):
                    place = high if half == 0 else 3 - high
                    rows.append(grid_ref[row : row + 32, place * 128 : place * 128 + 128])
                lanes.append(jnp.concatenate(rows, axis=0))
            joined = jnp.concatenate(lanes, axis=1)
            for part in range(4):
                perm = perm_ref[part * 128 : part * 128 + width, : groups * 128]
                moved = dot(joined, perm, NT).astype(BF16)
                for high in range(4):
                    start = ((half * 4 + high) * 4 + part) * 32
                    out_ref[start : start + 32, tile * 128 : tile * 128 + width] = moved[
                        high * 32 : high * 32 + 32, :
                    ]


def transform_pair(boundary, data, table, mix, north, south):
    vmem = pl.BlockSpec(memory_space=pltpu.VMEM)
    return pl.pallas_call(
        pair_kernel,
        out_shape=jax.ShapeDtypeStruct((1024, 576), BF16),
        in_specs=[pl.BlockSpec(memory_space=pltpu.SMEM)] + [vmem] * 5,
        out_specs=vmem,
        scratch_shapes=[
            pltpu.VMEM((576, 512), BF16),
            pltpu.VMEM((576, 512), BF16),
            pltpu.VMEM((576, 256), BF16),
            pltpu.VMEM((576, ROWS), BF16),
            pltpu.VMEM((576, ROWS), BF16),
            pltpu.VMEM((576, 512), BF16),
            pltpu.VMEM((576, 512), BF16),
        ],
        compiler_params=pltpu.CompilerParams(vmem_limit_bytes=40 * 1024 * 1024),
        cost_estimate=pl.CostEstimate(
            flops=5_000_000_000, bytes_accessed=6_000_000, transcendentals=0
        ),
    )(boundary, data, table, mix, north, south)


def lane_moves():
    row = lax.broadcasted_iota(jnp.int32, (512, 512), 0)
    column = lax.broadcasted_iota(jnp.int32, (512, 512), 1)
    part, f, lat, c = row >> 7, (row >> 6) & 1, (row >> 1) & 31, row & 1
    place = part * 32 + lat
    start = f * 256 + c * 128
    north = (column == start + place).astype(BF16)
    south = (column == start + 127 - place).astype(BF16)
    return north, south


def mixing_matrix(vertical):
    row = lax.broadcasted_iota(jnp.int32, (576, 144), 0)
    level = lax.broadcasted_iota(jnp.int32, (576, 144), 1)
    pick = (level == 9 * ((row >> 1) & 15) + (row >> 6)).astype(BF16)
    nothing = jnp.zeros_like(vertical[0])
    whole = jnp.concatenate(
        [
            jnp.concatenate([vertical[0], nothing], axis=1),
            jnp.concatenate([nothing, vertical[1]], axis=1),
        ],
        axis=0,
    )
    spread = dot(dot(pick, whole).astype(BF16), pick, NT).astype(BF16)
    r = lax.broadcasted_iota(jnp.int32, (576, 576), 0)
    q = lax.broadcasted_iota(jnp.int32, (576, 576), 1)
    same = (r & 33) == (q & 33)
    return jnp.where(same, spread, jnp.zeros((), BF16))


def per_device(fourier, row_length, wave_order, legendre, vertical):
    field_count = lax.axis_size("field")
    position = lax.axis_index("band") * field_count + lax.axis_index("field")
    wave_ids = lax.iota(jnp.int32, 1024)
    in_range = wave_ids[None, :] < jnp.minimum(1024, row_length // 2)[:, None]
    in_range = in_range[None, :, None, :]
    nothing = jnp.zeros((), BF16)
    ordering = jnp.stack([wave_order, 1023 - wave_order], axis=1).reshape(1024, 1)
    chosen = (ordering == wave_ids[None, :]).astype(BF16)
    masked = jnp.where(in_range, fourier, nothing).reshape(576, 1024)
    outgoing = lax.dot_general(chosen, masked, NT, preferred_element_type=BF16)
    arrived = lax.all_to_all(
        outgoing.reshape(512, 2, 576), ("band", "field"), split_axis=0, concat_axis=0, tiled=True
    ).reshape(1024, 576)
    boundary = 1024 - lax.dynamic_slice_in_dim(wave_order, position, 1)
    table = jnp.pad(legendre[0], ((0, ROWS - 1025), (0, 0)))
    north, south = lane_moves()
    mix = mixing_matrix(vertical)
    result = transform_pair(boundary, arrived, table, mix, north, south)
    back = lax.all_to_all(
        result.reshape(512, 2, 576), ("band", "field"), split_axis=0, concat_axis=0, tiled=True
    ).reshape(1024, 576)
    restored = lax.dot_general(
        back, chosen, (((0,), (0,)), ((), ())), preferred_element_type=BF16
    ).reshape(9, 32, 2, 1024)
    return jnp.where(in_range, restored, nothing)


def solution(mesh):
    placed = (P("field", "band", None, None), P("band"), P(), P(("band", "field"), None, None), P())
    return jax.shard_map(
        per_device,
        mesh=mesh,
        in_specs=placed,
        out_specs=P("field", "band", None, None),
        check_vma=False,
    )
```

```python
import functools

import jax
import jax.numpy as jnp
from jax import lax
from jax.experimental import pallas as pl
from jax.experimental.pallas import tpu as pltpu
from jax.sharding import PartitionSpec as P

BF16 = jnp.bfloat16
F32 = jnp.float32
ROWS = 1152
NT = (((1,), (1,)), ((), ()))
NN = (((1,), (0,)), ((), ()))


def dot(a, b, dims=NN):
    return lax.dot_general(a, b, dims, preferred_element_type=F32)


def pair_kernel(
    boundary_ref, data_ref, north_hbm, south_hbm, table_hbm, mix_hbm, out_ref,
    north_ref, south_ref, table_ref, mix_ref,
    value_n, value_s, spectral, updated, flipped, grid_n, grid_s, sems,
):
    copies = [
        pltpu.make_async_copy(source, target, sems.at[i])
        for i, (source, target) in enumerate(
            (
                (north_hbm, north_ref),
                (south_hbm, south_ref),
                (table_hbm, table_ref),
                (mix_hbm, mix_ref),
            )
        )
    ]
    for copy in copies:
        copy.start()
    copies[0].wait()
    copies[1].wait()
    halves = ((north_ref, value_n, grid_n, 0), (south_ref, value_s, grid_s, 1))

    def source(tile, half, part, width):
        rows = []
        for high in range(4):
            start = ((half * 4 + high) * 4 + part) * 16
            block = data_ref[start : start + 16, :, tile * 128 : tile * 128 + width]
            rows.append(block.reshape(32, width))
        return jnp.concatenate(rows, axis=0)

    for tile in range(5):
        width = 128 if tile < 4 else 64
        groups = width // 32
        for perm_ref, value_ref, _, half in halves:
            moved = jnp.zeros((128, groups * 128), F32)
            if width == 128:
                joined = jnp.concatenate(
                    [source(tile, half, part, width) for part in range(4)], axis=1
                )
                moved = dot(joined, perm_ref[...])
            else:
                for part in range(4):
                    moved += dot(
                        source(tile, half, part, width),
                        perm_ref[part * 128 : part * 128 + width, : groups * 128],
                    )
            moved = moved.astype(BF16)
            for high in range(4):
                place = high if half == 0 else 3 - high
                for group in range(groups):
                    row = (tile * 4 + group) * 32
                    value_ref[row : row + 32, place * 128 : place * 128 + 128] = moved[
                        high * 32 : high * 32 + 32, group * 128 : group * 128 + 128
                    ]

    copies[2].wait()
    copies[3].wait()
    boundary = boundary_ref[0]
    for start in range(0, ROWS, 256):
        size = min(256, ROWS - start)
        row_ids = lax.broadcasted_iota(jnp.int32, (1, size), 1) + start
        first = row_ids < boundary
        degree = jnp.where(first, row_ids, row_ids - boundary)
        parity = (1 - 2 * (degree & 1)).astype(F32)
        slots = lax.broadcasted_iota(jnp.int32, (576, size), 0) & 1
        owned = slots == jnp.where(first, 0, 1)
        table = table_ref[start : start + size, :]
        total = dot(value_n[...], table, NT) + parity * dot(value_s[...], table, NT)
        spectral[...] = jnp.zeros_like(spectral)
        spectral[:, :size] = jnp.where(owned, total, 0.0).astype(BF16)
        mixed = dot(mix_ref[...], spectral[:, :size])
        updated[:, start : start + size] = mixed.astype(BF16)
        flipped[:, start : start + size] = (mixed * parity).astype(BF16)

    grid_n[...] = dot(updated[...], table_ref[...]).astype(BF16)
    grid_s[...] = dot(flipped[...], table_ref[...]).astype(BF16)

    for tile in range(5):
        width = 128 if tile < 4 else 64
        groups = width // 32
        for perm_ref, _, grid_ref, half in halves:
            lanes = []
            for group in range(groups):
                row = (tile * 4 + group) * 32
                rows = []
                for high in range(4):
                    place = high if half == 0 else 3 - high
                    rows.append(grid_ref[row : row + 32, place * 128 : place * 128 + 128])
                lanes.append(jnp.concatenate(rows, axis=0))
            joined = jnp.concatenate(lanes, axis=1)
            for part in range(4):
                perm = perm_ref[part * 128 : part * 128 + width, : groups * 128]
                moved = dot(joined, perm, NT).astype(BF16)
                for high in range(4):
                    start = ((half * 4 + high) * 4 + part) * 16
                    block = moved[high * 32 : high * 32 + 32, :].reshape(16, 2, width)
                    out_ref[start : start + 16, :, tile * 128 : tile * 128 + width] = block


def transform_pair(boundary, data, north, south, table, mix):
    return pl.pallas_call(
        pair_kernel,
        out_shape=jax.ShapeDtypeStruct((512, 2, 576), BF16),
        in_specs=[pl.BlockSpec(memory_space=pltpu.SMEM), VMEM, HBM, HBM, HBM, HBM],
        out_specs=VMEM,
        scratch_shapes=[
            pltpu.VMEM((512, 512), BF16),
            pltpu.VMEM((512, 512), BF16),
            pltpu.VMEM((ROWS, 512), BF16),
            pltpu.VMEM((576, 576), BF16),
            pltpu.VMEM((576, 512), BF16),
            pltpu.VMEM((576, 512), BF16),
            pltpu.VMEM((576, 256), BF16),
            pltpu.VMEM((576, ROWS), BF16),
            pltpu.VMEM((576, ROWS), BF16),
            pltpu.VMEM((576, 512), BF16),
            pltpu.VMEM((576, 512), BF16),
            pltpu.SemaphoreType.DMA((4,)),
        ],
        compiler_params=pltpu.CompilerParams(vmem_limit_bytes=16 * 1024 * 1024),
        cost_estimate=pl.CostEstimate(
            flops=5_000_000_000, bytes_accessed=6_000_000, transcendentals=0
        ),
    )(boundary, data, *(pltpu.with_memory_space_constraint(x, pltpu.HBM) for x in (north, south, table, mix)))


def lane_moves():
    row = lax.broadcasted_iota(jnp.int32, (512, 512), 0)
    column = lax.broadcasted_iota(jnp.int32, (512, 512), 1)
    part, f, lat, c = row >> 7, (row >> 6) & 1, (row >> 1) & 31, row & 1
    place = part * 32 + lat
    start = f * 256 + c * 128
    north = (column == start + place).astype(BF16)
    south = (column == start + 127 - place).astype(BF16)
    return north, south


def mixing_matrix(vertical):
    row = lax.broadcasted_iota(jnp.int32, (576, 144), 0)
    level = lax.broadcasted_iota(jnp.int32, (576, 144), 1)
    pick = (level == 9 * ((row >> 1) & 15) + (row >> 6)).astype(BF16)
    nothing = jnp.zeros_like(vertical[0])
    whole = jnp.concatenate(
        [
            jnp.concatenate([vertical[0], nothing], axis=1),
            jnp.concatenate([nothing, vertical[1]], axis=1),
        ],
        axis=0,
    )
    spread = dot(dot(pick, whole).astype(BF16), pick, NT).astype(BF16)
    r = lax.broadcasted_iota(jnp.int32, (576, 576), 0)
    q = lax.broadcasted_iota(jnp.int32, (576, 576), 1)
    same = (r & 33) == (q & 33)
    return jnp.where(same, spread, jnp.zeros((), BF16))


def column_of(values, rows):
    count = values.shape[1]
    row = lax.broadcasted_iota(jnp.int32, (16, count), 0)
    digits = jnp.where(row == 0, values >> 5, jnp.where(row == 1, values & 31, 0))
    row = lax.broadcasted_iota(jnp.int32, (rows, count), 0)
    lane = lax.broadcasted_iota(jnp.int32, (rows, count), 1)
    repeat = jnp.where((row >> 1) == lane, 1.0, 0.0).astype(BF16)
    columns = dot(repeat, digits.astype(F32).astype(BF16), NT)
    return columns[:, 0:1] * 32.0 + columns[:, 1:2]


def wave_mask(row_length_ref):
    count = jnp.minimum(1024, row_length_ref[...] >> 1)
    limit = column_of(count, 64).astype(jnp.int32)
    return lax.broadcasted_iota(jnp.int32, (64, 1024), 1) < limit


def order_kernel(
    length_hbm, order_hbm, fourier_hbm, out_hbm, chosen_ref,
    lengths, order, raw, masked, out, in_sems, out_sems,
):
    copies = [
        pltpu.make_async_copy(source, target, in_sems.at[i])
        for i, (source, target) in enumerate(
            ((order_hbm, order), (length_hbm, lengths), (fourier_hbm, raw))
        )
    ]
    for copy in copies:
        copy.start()
    wave_ids = lax.broadcasted_iota(jnp.int32, (256, 1024), 1)
    odd = (lax.broadcasted_iota(jnp.int32, (256, 1), 0) & 1) == 1
    copies[0].wait()
    for block in range(4):
        wave = column_of(order[:, block * 128 : block * 128 + 128], 256).astype(jnp.int32)
        wave = jnp.where(odd, 1023 - wave, wave)
        picked = jnp.where(wave_ids == wave, 1.0, 0.0).astype(BF16)
        chosen_ref[block * 256 : block * 256 + 256, :] = picked
    copies[1].wait()
    in_range = wave_mask(lengths)
    copies[2].wait()
    for f in range(9):
        kept = jnp.where(in_range, raw[f].reshape(64, 1024), jnp.zeros((), BF16))
        masked[f * 64 : f * 64 + 64, :] = kept
    sent = []
    for block in range(4):
        sorted_rows = dot(chosen_ref[block * 256 : block * 256 + 256, :], masked[...], NT)
        part = slice(block * 128, block * 128 + 128)
        out[part] = sorted_rows.astype(BF16).reshape(128, 2, 576)
        copy = pltpu.make_async_copy(out.at[part], out_hbm.at[part], out_sems.at[block])
        copy.start()
        sent.append(copy)
    for copy in sent:
        copy.wait()


def restore_kernel(length_ref, chosen_ref, data_ref, out_hbm, turned, out, sems):
    in_range = wave_mask(length_ref)
    for block in range(8):
        rows = data_ref[block * 64 : block * 64 + 64].reshape(128, 576)
        turned[:, block * 128 : block * 128 + 128] = rows.T
    sent = []
    for start, size in ((0, 4), (4, 4), (8, 1)):
        restored = dot(turned[start * 64 : (start + size) * 64, :], chosen_ref[...])
        for f in range(size):
            kept = jnp.where(in_range, restored[f * 64 : f * 64 + 64, :], 0.0).astype(BF16)
            out[start + f] = kept.reshape(32, 2, 1024)
        part = slice(start, start + size)
        copy = pltpu.make_async_copy(out.at[part], out_hbm.at[part], sems.at[len(sent)])
        copy.start()
        sent.append(copy)
    for copy in sent:
        copy.wait()


VMEM = pl.BlockSpec(memory_space=pltpu.VMEM)
HBM = pl.BlockSpec(memory_space=pltpu.HBM)


def order_pairs(row_length, wave_order, fourier):
    return pl.pallas_call(
        order_kernel,
        out_shape=(
            pltpu.HBM((512, 2, 576), BF16),
            pltpu.VMEM((1024, 1024), BF16),
        ),
        in_specs=[HBM, HBM, HBM],
        out_specs=(HBM, VMEM),
        scratch_shapes=[
            pltpu.VMEM((1, 32), jnp.int32),
            pltpu.VMEM((1, 512), jnp.int32),
            pltpu.VMEM((9, 32, 2, 1024), BF16),
            pltpu.VMEM((576, 1024), BF16),
            pltpu.VMEM((512, 2, 576), BF16),
            pltpu.SemaphoreType.DMA((3,)),
            pltpu.SemaphoreType.DMA((4,)),
        ],
        compiler_params=pltpu.CompilerParams(vmem_limit_bytes=16 * 1024 * 1024),
    )(*(pltpu.with_memory_space_constraint(x, pltpu.HBM) for x in (row_length, wave_order, fourier)))


def restore_waves(row_length, chosen, data):
    return pl.pallas_call(
        restore_kernel,
        out_shape=jax.ShapeDtypeStruct((9, 32, 2, 1024), BF16),
        in_specs=[VMEM, VMEM, VMEM],
        out_specs=HBM,
        scratch_shapes=[
            pltpu.VMEM((576, 1024), BF16),
            pltpu.VMEM((9, 32, 2, 1024), BF16),
            pltpu.SemaphoreType.DMA((3,)),
        ],
        compiler_params=pltpu.CompilerParams(vmem_limit_bytes=16 * 1024 * 1024),
    )(row_length, chosen, data)


def exchange(chunks):
    return lax.all_to_all(chunks, ("band", "field"), split_axis=0, concat_axis=0, tiled=True)


def per_device(fourier, row_length, wave_order, legendre, vertical):
    position = lax.axis_index("band") * lax.axis_size("field") + lax.axis_index("field")
    lengths = row_length.reshape(1, 32)
    outgoing, chosen = order_pairs(lengths, wave_order.reshape(1, 512), fourier)
    arrived = exchange(outgoing)
    boundary = 1024 - lax.dynamic_slice_in_dim(wave_order, position, 1)
    table = jnp.pad(legendre[0], ((0, ROWS - 1025), (0, 0)))
    north, south = lane_moves()
    mix = mixing_matrix(vertical)
    result = transform_pair(boundary, arrived, north, south, table, mix)
    return restore_waves(lengths, chosen, exchange(result))


def solution(mesh):
    placed = (P("field", "band", None, None), P("band"), P(), P(("band", "field"), None, None), P())
    return jax.shard_map(
        per_device,
        mesh=mesh,
        in_specs=placed,
        out_specs=P("field", "band", None, None),
        check_vma=False,
    )
```

```python
import functools

import jax
import jax.numpy as jnp
from jax import lax
from jax.experimental import pallas as pl
from jax.experimental.pallas import tpu as pltpu
from jax.sharding import PartitionSpec as P

BF16 = jnp.bfloat16
F32 = jnp.float32
ROWS = 1152
EVEN = 640
NT = (((1,), (1,)), ((), ()))
NN = (((1,), (0,)), ((), ()))


def dot(a, b, dims=NN):
    return lax.dot_general(a, b, dims, preferred_element_type=F32)


def prepare_kernel(
    boundary_ref, legendre_ref, vertical_ref,
    north_ref, south_ref, north_back, south_back, table_ref, table_t, mix_ref, padded,
):
    row = lax.broadcasted_iota(jnp.int32, (512, 512), 0)
    column = lax.broadcasted_iota(jnp.int32, (512, 512), 1)
    for a, b, north, south in ((row, column, north_ref, south_ref), (column, row, north_back, south_back)):
        place = (a >> 7) * 32 + ((a >> 1) & 31)
        start = ((a >> 6) & 1) * 256 + (a & 1) * 128
        north[...] = jnp.where(b == start + place, 1.0, 0.0).astype(BF16)
        south[...] = jnp.where(b == start + 127 - place, 1.0, 0.0).astype(BF16)
    padded[:1024, :] = legendre_ref[:1024, :]
    last = jnp.broadcast_to(legendre_ref[1024:1025, :].astype(F32), (128, 512))
    tail = lax.broadcasted_iota(jnp.int32, (128, 512), 0)
    padded[1024:, :] = jnp.where(tail == 0, last, 0.0).astype(BF16)
    boundary = boundary_ref[0]
    for start in range(0, ROWS, 128):
        odd = 1 if start >= EVEN else 0
        rank = lax.broadcasted_iota(jnp.int32, (128, 1), 0) + (start - odd * EVEN)
        first = (boundary + 1 - odd) >> 1
        source = jnp.where(rank < first, 2 * rank, boundary + 2 * (rank - first)) + odd
        ids = lax.broadcasted_iota(jnp.int32, (128, ROWS), 1)
        pick = jnp.where(ids == source, 1.0, 0.0).astype(BF16)
        rows = dot(pick, padded[...])
        table_ref[start : start + 128, :] = rows.astype(BF16)
        table_t[:, start : start + 128] = rows.T.astype(BF16)
    row = lax.broadcasted_iota(jnp.int32, (144, 72), 0)
    level = lax.broadcasted_iota(jnp.int32, (144, 72), 1)
    pick = jnp.where(level == 9 * ((row >> 1) & 7) + (row >> 4), 1.0, 0.0).astype(BF16)
    row = lax.broadcasted_iota(jnp.int32, (144, 144), 0)
    column = lax.broadcasted_iota(jnp.int32, (144, 144), 1)
    same = (row & 1) == (column & 1)
    for kind in range(2):
        spread = dot(dot(pick, vertical_ref[kind]).astype(BF16), pick, NT)
        mix_ref[kind] = jnp.where(same, spread, 0.0).astype(BF16)


def pair_kernel(
    boundary_ref, data_ref, *refs
):
    hbm, out_ref, held = refs[:7], refs[7], refs[8:15]
    stage_n, stage_s, value_n, value_s, spectral, updated, sems = refs[15:]
    north_ref, south_ref, north_back, south_back, table_ref, table_t, mix_ref = held
    copies = [
        pltpu.make_async_copy(source, target, sems.at[i])
        for i, (source, target) in enumerate(zip(hbm, held))
    ]
    for i in (0, 1, 5, 6, 4, 2, 3):
        copies[i].start()

    def band(half, high, part):
        return ((half * (7 - 2 * high) + high) * 4 + part) * 16

    stages = ((0, stage_n, north_ref, north_back), (1, stage_s, south_ref, south_back))
    for half, stage, _, _ in stages:
        for tile in range(5):
            width = 128 if tile < 4 else 64
            for high in range(4):
                row = (tile * 4 + high) * 32
                for part in range(4):
                    start = band(half, high, part)
                    block = data_ref[start : start + 16, :, tile * 128 : tile * 128 + width]
                    column = part * 128
                    stage[row : row + 32, column : column + width] = block.reshape(32, width)
                    if width == 64:
                        stage[row : row + 32, column + 64 : column + 128] = jnp.zeros((32, 64), BF16)

    pieces = []
    for tile in range(5):
        for group in range(4):
            f, c = tile * 2 + (group >> 1), group & 1
            if f < 9:
                for kind in range(2):
                    pieces.append((tile, group, kind, ((c * 2 + kind) * 9 + f) * 16))

    copies[0].wait()
    copies[1].wait()
    for start in range(0, 640, 128):
        for stage, perm_ref, target in (
            (stage_n, north_ref, value_n), (stage_s, south_ref, value_s)
        ):
            moved = dot(stage[start : start + 128, :], perm_ref[...]).astype(BF16)
            for tile, group, kind, row in pieces:
                if tile * 128 == start:
                    for high in range(4):
                        source = high * 32 + kind * 16
                        target[row : row + 16, high * 128 : high * 128 + 128] = moved[
                            source : source + 16, group * 128 : group * 128 + 128
                        ]

    for i in (5, 6, 4, 2, 3):
        copies[i].wait()
    boundary = boundary_ref[0]
    for odd in range(2):
        low, high = (EVEN, ROWS) if odd else (0, EVEN)
        first = (boundary + 1 - odd) >> 1
        for start in range(low, high, 256):
            size = min(256, high - start)
            rank = lax.broadcasted_iota(jnp.int32, (1, size), 1) + (start - low)
            slots = lax.broadcasted_iota(jnp.int32, (576, size), 0) & 1
            owned = slots == jnp.where(rank < first, 0, 1)
            north = dot(value_n[...], table_t[:, start : start + size])
            south = dot(value_s[...], table_t[:, start : start + size])
            total = north - south if odd else north + south
            spectral[:, start : start + size] = jnp.where(owned, total, 0.0).astype(BF16)
    for block in range(4):
        rows = slice(block * 144, block * 144 + 144)
        updated[rows, :] = dot(mix_ref[block & 1], spectral[rows, :]).astype(BF16)

    for block in range(4):
        rows = slice(block * 144, block * 144 + 144)
        grid_e = dot(updated[rows, :EVEN], table_ref[:EVEN, :])
        grid_o = dot(updated[rows, EVEN:], table_ref[EVEN:, :])
        for stage, grid in ((stage_n, grid_e + grid_o), (stage_s, grid_e - grid_o)):
            grid = grid.astype(BF16)
            for tile, group, kind, row in pieces:
                if row // 144 == block:
                    for high in range(4):
                        target = (tile * 4 + high) * 32 + kind * 16
                        stage[target : target + 16, group * 128 : group * 128 + 128] = grid[
                            row - block * 144 : row - block * 144 + 16, high * 128 : high * 128 + 128
                        ]
    for stage in (stage_n, stage_s):
        stage[512:, 256:] = jnp.zeros((128, 256), BF16)
    for half, stage, _, back_ref in stages:
        for tile in range(5):
            width = 128 if tile < 4 else 64
            moved = dot(stage[tile * 128 : tile * 128 + 128, :], back_ref[...]).astype(BF16)
            for high in range(4):
                for part in range(4):
                    start = band(half, high, part)
                    block = moved[high * 32 : high * 32 + 32, part * 128 : part * 128 + width]
                    out_ref[start : start + 16, :, tile * 128 : tile * 128 + width] = block.reshape(
                        16, 2, width
                    )


VMEM = pl.BlockSpec(memory_space=pltpu.VMEM)
HBM = pl.BlockSpec(memory_space=pltpu.HBM)
SMEM = pl.BlockSpec(memory_space=pltpu.SMEM)
PREPARED = ((512, 512), (512, 512), (512, 512), (512, 512), (ROWS, 512), (512, ROWS), (2, 144, 144))


def prepare(boundary, legendre, vertical):
    return pl.pallas_call(
        prepare_kernel,
        out_shape=[pltpu.HBM(shape, BF16) for shape in PREPARED],
        in_specs=[SMEM, VMEM, VMEM],
        out_specs=[VMEM] * len(PREPARED),
        scratch_shapes=[pltpu.VMEM((ROWS, 512), BF16)],
        compiler_params=pltpu.CompilerParams(vmem_limit_bytes=20 * 1024 * 1024),
        cost_estimate=pl.CostEstimate(
            flops=2_000_000_000, bytes_accessed=6_000_000, transcendentals=0
        ),
    )(boundary, legendre, vertical)


def transform_pair(boundary, data, *prepared):
    return pl.pallas_call(
        pair_kernel,
        out_shape=jax.ShapeDtypeStruct((512, 2, 576), BF16),
        in_specs=[SMEM, VMEM] + [HBM] * len(PREPARED),
        out_specs=VMEM,
        scratch_shapes=[pltpu.VMEM(shape, BF16) for shape in PREPARED]
        + [
            pltpu.VMEM((640, 512), BF16),
            pltpu.VMEM((640, 512), BF16),
            pltpu.VMEM((576, 512), BF16),
            pltpu.VMEM((576, 512), BF16),
            pltpu.VMEM((576, ROWS), BF16),
            pltpu.VMEM((576, ROWS), BF16),
            pltpu.SemaphoreType.DMA((7,)),
        ],
        compiler_params=pltpu.CompilerParams(vmem_limit_bytes=20 * 1024 * 1024),
        cost_estimate=pl.CostEstimate(
            flops=5_000_000_000, bytes_accessed=6_000_000, transcendentals=0
        ),
    )(boundary, data, *(pltpu.with_memory_space_constraint(x, pltpu.HBM) for x in prepared))


def column_of(values, rows):
    count = values.shape[1]
    row = lax.broadcasted_iota(jnp.int32, (16, count), 0)
    digits = jnp.where(row == 0, values >> 5, jnp.where(row == 1, values & 31, 0))
    row = lax.broadcasted_iota(jnp.int32, (rows, count), 0)
    lane = lax.broadcasted_iota(jnp.int32, (rows, count), 1)
    repeat = jnp.where((row >> 1) == lane, 1.0, 0.0).astype(BF16)
    columns = dot(repeat, digits.astype(F32).astype(BF16), NT)
    return columns[:, 0:1] * 32.0 + columns[:, 1:2]


def wave_mask(row_length_ref):
    count = jnp.minimum(1024, row_length_ref[...] >> 1)
    limit = column_of(count, 64).astype(jnp.int32)
    return lax.broadcasted_iota(jnp.int32, (64, 1024), 1) < limit


def order_kernel(
    length_hbm, order_hbm, fourier_hbm, out_hbm, chosen_ref,
    lengths, order, raw, masked, out, in_sems, out_sems,
):
    copies = [
        pltpu.make_async_copy(source, target, in_sems.at[i])
        for i, (source, target) in enumerate(
            ((order_hbm, order), (length_hbm, lengths), (fourier_hbm, raw))
        )
    ]
    for copy in copies:
        copy.start()
    wave_ids = lax.broadcasted_iota(jnp.int32, (256, 1024), 1).astype(jnp.int16)
    odd = (lax.broadcasted_iota(jnp.int32, (256, 1), 0) & 1) == 1
    copies[0].wait()
    for block in range(4):
        wave = column_of(order[:, block * 128 : block * 128 + 128], 256).astype(jnp.int32)
        wave = jnp.where(odd, 1023 - wave, wave).astype(jnp.int16)
        picked = jnp.where(wave_ids == wave, jnp.ones((), BF16), jnp.zeros((), BF16))
        chosen_ref[block * 256 : block * 256 + 256, :] = picked
    copies[1].wait()
    in_range = wave_mask(lengths)
    copies[2].wait()
    for f in range(9):
        kept = jnp.where(in_range, raw[f].reshape(64, 1024), jnp.zeros((), BF16))
        masked[f * 64 : f * 64 + 64, :] = kept
    sent = []
    for block in range(4):
        sorted_rows = dot(chosen_ref[block * 256 : block * 256 + 256, :], masked[...], NT)
        part = slice(block * 128, block * 128 + 128)
        out[part] = sorted_rows.astype(BF16).reshape(128, 2, 576)
        copy = pltpu.make_async_copy(out.at[part], out_hbm.at[part], out_sems.at[block])
        copy.start()
        sent.append(copy)
    for copy in sent:
        copy.wait()


def restore_kernel(length_ref, chosen_ref, data_ref, out_hbm, turned, out, sems):
    in_range = wave_mask(length_ref)
    for block in range(8):
        rows = data_ref[block * 64 : block * 64 + 64].reshape(128, 576)
        turned[:, block * 128 : block * 128 + 128] = rows.T
    sent = []
    for start, size in ((0, 4), (4, 4), (8, 1)):
        restored = dot(turned[start * 64 : (start + size) * 64, :], chosen_ref[...])
        for f in range(size):
            kept = jnp.where(in_range, restored[f * 64 : f * 64 + 64, :], 0.0).astype(BF16)
            out[start + f] = kept.reshape(32, 2, 1024)
        part = slice(start, start + size)
        copy = pltpu.make_async_copy(out.at[part], out_hbm.at[part], sems.at[len(sent)])
        copy.start()
        sent.append(copy)
    for copy in sent:
        copy.wait()


def order_pairs(row_length, wave_order, fourier):
    return pl.pallas_call(
        order_kernel,
        out_shape=(
            pltpu.HBM((512, 2, 576), BF16),
            pltpu.VMEM((1024, 1024), BF16),
        ),
        in_specs=[HBM, HBM, HBM],
        out_specs=(HBM, VMEM),
        scratch_shapes=[
            pltpu.VMEM((1, 32), jnp.int32),
            pltpu.VMEM((1, 512), jnp.int32),
            pltpu.VMEM((9, 32, 2, 1024), BF16),
            pltpu.VMEM((576, 1024), BF16),
            pltpu.VMEM((512, 2, 576), BF16),
            pltpu.SemaphoreType.DMA((3,)),
            pltpu.SemaphoreType.DMA((4,)),
        ],
        compiler_params=pltpu.CompilerParams(vmem_limit_bytes=16 * 1024 * 1024),
    )(*(pltpu.with_memory_space_constraint(x, pltpu.HBM) for x in (row_length, wave_order, fourier)))


def restore_waves(row_length, chosen, data):
    return pl.pallas_call(
        restore_kernel,
        out_shape=jax.ShapeDtypeStruct((9, 32, 2, 1024), BF16),
        in_specs=[VMEM, VMEM, VMEM],
        out_specs=HBM,
        scratch_shapes=[
            pltpu.VMEM((576, 1024), BF16),
            pltpu.VMEM((9, 32, 2, 1024), BF16),
            pltpu.SemaphoreType.DMA((3,)),
        ],
        compiler_params=pltpu.CompilerParams(vmem_limit_bytes=16 * 1024 * 1024),
    )(row_length, chosen, data)


def exchange(chunks):
    return lax.all_to_all(chunks, ("band", "field"), split_axis=0, concat_axis=0, tiled=True)


def per_device(fourier, row_length, wave_order, legendre, vertical):
    position = lax.axis_index("band") * lax.axis_size("field") + lax.axis_index("field")
    lengths = row_length.reshape(1, 32)
    outgoing, chosen = order_pairs(lengths, wave_order.reshape(1, 512), fourier)
    arrived = exchange(outgoing)
    boundary = 1024 - lax.dynamic_slice_in_dim(wave_order, position, 1)
    result = transform_pair(boundary, arrived, *prepare(boundary, legendre[0], vertical))
    return restore_waves(lengths, chosen, exchange(result))


def solution(mesh):
    placed = (P("field", "band", None, None), P("band"), P(), P(("band", "field"), None, None), P())
    return jax.shard_map(
        per_device,
        mesh=mesh,
        in_specs=placed,
        out_specs=P("field", "band", None, None),
        check_vma=False,
    )
```

```python
import functools

import jax
import jax.numpy as jnp
from jax import lax
from jax.experimental import pallas as pl
from jax.experimental.pallas import tpu as pltpu
from jax.sharding import PartitionSpec as P

BF16 = jnp.bfloat16
F32 = jnp.float32
ROWS = 1152
EVEN = 640
NT = (((1,), (1,)), ((), ()))
NN = (((1,), (0,)), ((), ()))


def dot(a, b, dims=NN):
    return lax.dot_general(a, b, dims, preferred_element_type=F32)


def prepare_kernel(
    boundary_ref, legendre_hbm, north_ref, table_ref, legendre_ref, padded, sem
):
    copy = pltpu.make_async_copy(legendre_hbm, legendre_ref, sem)
    copy.start()
    row = lax.broadcasted_iota(jnp.int32, (512, 512), 0)
    column = lax.broadcasted_iota(jnp.int32, (512, 512), 1)
    place = (row >> 7) * 32 + ((row >> 1) & 31)
    start = ((row >> 6) & 1) * 256 + (row & 1) * 128
    north_ref[...] = jnp.where(column == start + place, 1.0, 0.0).astype(BF16)
    copy.wait()
    padded[:1024, :] = legendre_ref[:1024, :]
    last = jnp.broadcast_to(legendre_ref[1024:1025, :].astype(F32), (128, 512))
    tail = lax.broadcasted_iota(jnp.int32, (128, 512), 0)
    padded[1024:, :] = jnp.where(tail == 0, last, 0.0).astype(BF16)
    boundary = boundary_ref[0]
    for start in range(0, ROWS, 128):
        odd = 1 if start >= EVEN else 0
        rank = lax.broadcasted_iota(jnp.int32, (128, 1), 0) + (start - odd * EVEN)
        first = (boundary + 1 - odd) >> 1
        source = jnp.where(rank < first, 2 * rank, boundary + 2 * (rank - first)) + odd
        ids = lax.broadcasted_iota(jnp.int32, (128, ROWS), 1)
        pick = jnp.where(ids == source, 1.0, 0.0).astype(BF16)
        table_ref[start : start + 128, :] = dot(pick, padded[...]).astype(BF16)


def mixing(vertical_ref, mix_ref):
    row = lax.broadcasted_iota(jnp.int32, (144, 72), 0)
    level = lax.broadcasted_iota(jnp.int32, (144, 72), 1)
    pick = jnp.where(level == 9 * ((row >> 1) & 7) + (row >> 4), 1.0, 0.0).astype(BF16)
    row = lax.broadcasted_iota(jnp.int32, (144, 144), 0)
    column = lax.broadcasted_iota(jnp.int32, (144, 144), 1)
    same = (row & 1) == (column & 1)
    for kind in range(2):
        spread = dot(dot(pick, vertical_ref[kind]).astype(BF16), pick, NT)
        mix_ref[kind] = jnp.where(same, spread, 0.0).astype(BF16)


def pair_kernel(
    boundary_ref, data_ref, vertical_ref, north_ref, table_ref, out_ref,
    stage_n, stage_s, value_n, value_s, spectral, updated, mix_ref, south_ref,
):
    mixing(vertical_ref, mix_ref)
    row = lax.broadcasted_iota(jnp.int32, (512, 1), 0)
    place = (row >> 7) * 32 + ((row >> 1) & 31)
    goal = ((row >> 6) & 1) * 256 + (row & 1) * 128 + 127 - place
    column = lax.broadcasted_iota(jnp.int32, (512, 512), 1).astype(jnp.int16)
    one, nothing = jnp.ones((), BF16), jnp.zeros((), BF16)
    south_ref[...] = jnp.where(column == goal.astype(jnp.int16), one, nothing)

    def band(half, high, part):
        return ((half * (7 - 2 * high) + high) * 4 + part) * 16

    stages = ((0, stage_n, north_ref), (1, stage_s, south_ref))
    for half, stage, _ in stages:
        for tile in range(5):
            width = 128 if tile < 4 else 64
            for high in range(4):
                row = (tile * 4 + high) * 32
                for part in range(4):
                    start = band(half, high, part)
                    block = data_ref[start : start + 16, :, tile * 128 : tile * 128 + width]
                    column = part * 128
                    stage[row : row + 32, column : column + width] = block.reshape(32, width)
                    if width == 64:
                        stage[row : row + 32, column + 64 : column + 128] = jnp.zeros((32, 64), BF16)

    pieces = []
    for tile in range(5):
        for group in range(4):
            f, c = tile * 2 + (group >> 1), group & 1
            if f < 9:
                for kind in range(2):
                    pieces.append((tile, group, kind, ((c * 2 + kind) * 9 + f) * 16))

    for start in range(0, 640, 128):
        for stage, perm_ref, target in (
            (stage_n, north_ref, value_n), (stage_s, south_ref, value_s)
        ):
            moved = dot(stage[start : start + 128, :], perm_ref[...]).astype(BF16)
            for tile, group, kind, row in pieces:
                if tile * 128 == start:
                    for high in range(4):
                        source = high * 32 + kind * 16
                        target[row : row + 16, high * 128 : high * 128 + 128] = moved[
                            source : source + 16, group * 128 : group * 128 + 128
                        ]

    boundary = boundary_ref[0]
    for odd in range(2):
        low, high = (EVEN, ROWS) if odd else (0, EVEN)
        first = (boundary + 1 - odd) >> 1
        for start in range(low, high, 256):
            size = min(256, high - start)
            rank = lax.broadcasted_iota(jnp.int32, (1, size), 1) + (start - low)
            slots = lax.broadcasted_iota(jnp.int32, (576, size), 0) & 1
            owned = slots == jnp.where(rank < first, 0, 1)
            north = dot(value_n[...], table_ref[start : start + size, :], NT)
            south = dot(value_s[...], table_ref[start : start + size, :], NT)
            total = north - south if odd else north + south
            spectral[:, start : start + size] = jnp.where(owned, total, 0.0).astype(BF16)
    for block in range(4):
        rows = slice(block * 144, block * 144 + 144)
        updated[rows, :] = dot(mix_ref[block & 1], spectral[rows, :]).astype(BF16)

    for block in range(4):
        rows = slice(block * 144, block * 144 + 144)
        grid_e = dot(updated[rows, :EVEN], table_ref[:EVEN, :])
        grid_o = dot(updated[rows, EVEN:], table_ref[EVEN:, :])
        for stage, grid in ((stage_n, grid_e + grid_o), (stage_s, grid_e - grid_o)):
            grid = grid.astype(BF16)
            for tile, group, kind, row in pieces:
                if row // 144 == block:
                    for high in range(4):
                        target = (tile * 4 + high) * 32 + kind * 16
                        stage[target : target + 16, group * 128 : group * 128 + 128] = grid[
                            row - block * 144 : row - block * 144 + 16, high * 128 : high * 128 + 128
                        ]
    for stage in (stage_n, stage_s):
        stage[512:, 256:] = jnp.zeros((128, 256), BF16)
    for half, stage, perm_ref in stages:
        for tile in range(5):
            width = 128 if tile < 4 else 64
            moved = dot(stage[tile * 128 : tile * 128 + 128, :], perm_ref[...], NT).astype(BF16)
            for high in range(4):
                for part in range(4):
                    start = band(half, high, part)
                    block = moved[high * 32 : high * 32 + 32, part * 128 : part * 128 + width]
                    out_ref[start : start + 16, :, tile * 128 : tile * 128 + width] = block.reshape(
                        16, 2, width
                    )


VMEM = pl.BlockSpec(memory_space=pltpu.VMEM)
HBM = pl.BlockSpec(memory_space=pltpu.HBM)
SMEM = pl.BlockSpec(memory_space=pltpu.SMEM)
PREPARED = ((512, 512), (ROWS, 512))


def prepare(boundary, legendre):
    return pl.pallas_call(
        prepare_kernel,
        out_shape=[pltpu.VMEM(shape, BF16) for shape in PREPARED],
        in_specs=[SMEM, HBM],
        out_specs=[VMEM] * len(PREPARED),
        scratch_shapes=[
            pltpu.VMEM((1025, 512), BF16),
            pltpu.VMEM((ROWS, 512), BF16),
            pltpu.SemaphoreType.DMA,
        ],
        compiler_params=pltpu.CompilerParams(vmem_limit_bytes=20 * 1024 * 1024),
        cost_estimate=pl.CostEstimate(
            flops=2_000_000_000, bytes_accessed=6_000_000, transcendentals=0
        ),
    )(boundary, pltpu.with_memory_space_constraint(legendre, pltpu.HBM))


def transform_pair(boundary, data, vertical, *prepared):
    return pl.pallas_call(
        pair_kernel,
        out_shape=jax.ShapeDtypeStruct((512, 2, 576), BF16),
        in_specs=[SMEM] + [VMEM] * 4,
        out_specs=VMEM,
        scratch_shapes=[
            pltpu.VMEM((640, 512), BF16),
            pltpu.VMEM((640, 512), BF16),
            pltpu.VMEM((576, 512), BF16),
            pltpu.VMEM((576, 512), BF16),
            pltpu.VMEM((576, ROWS), BF16),
            pltpu.VMEM((576, ROWS), BF16),
            pltpu.VMEM((2, 144, 144), BF16),
            pltpu.VMEM((512, 512), BF16),
        ],
        compiler_params=pltpu.CompilerParams(vmem_limit_bytes=20 * 1024 * 1024),
        cost_estimate=pl.CostEstimate(
            flops=5_000_000_000, bytes_accessed=6_000_000, transcendentals=0
        ),
    )(boundary, data, vertical, *prepared)


def column_of(values, rows):
    count = values.shape[1]
    row = lax.broadcasted_iota(jnp.int32, (16, count), 0)
    digits = jnp.where(row == 0, values >> 5, jnp.where(row == 1, values & 31, 0))
    row = lax.broadcasted_iota(jnp.int32, (rows, count), 0)
    lane = lax.broadcasted_iota(jnp.int32, (rows, count), 1)
    repeat = jnp.where((row >> 1) == lane, 1.0, 0.0).astype(BF16)
    columns = dot(repeat, digits.astype(F32).astype(BF16), NT)
    return columns[:, 0:1] * 32.0 + columns[:, 1:2]


def wave_mask(row_length_ref):
    count = jnp.minimum(1024, row_length_ref[...] >> 1)
    limit = column_of(count, 64).astype(jnp.int32)
    return lax.broadcasted_iota(jnp.int32, (64, 1024), 1) < limit


def order_kernel(
    length_hbm, order_hbm, fourier_hbm, out_hbm, chosen_hbm,
    lengths, order, raw, masked, out, chosen_ref, in_sems, out_sems,
):
    copies = [
        pltpu.make_async_copy(source, target, in_sems.at[i])
        for i, (source, target) in enumerate(
            ((order_hbm, order), (length_hbm, lengths), (fourier_hbm, raw))
        )
    ]
    for copy in copies:
        copy.start()
    wave_ids = lax.broadcasted_iota(jnp.int32, (256, 1024), 1).astype(jnp.int16)
    odd = (lax.broadcasted_iota(jnp.int32, (256, 1), 0) & 1) == 1
    copies[0].wait()
    for block in range(4):
        wave = column_of(order[:, block * 128 : block * 128 + 128], 256).astype(jnp.int32)
        wave = jnp.where(odd, 1023 - wave, wave).astype(jnp.int16)
        picked = jnp.where(wave_ids == wave, jnp.ones((), BF16), jnp.zeros((), BF16))
        chosen_ref[block * 256 : block * 256 + 256, :] = picked
    kept_choice = pltpu.make_async_copy(chosen_ref, chosen_hbm, in_sems.at[3])
    kept_choice.start()
    copies[1].wait()
    in_range = wave_mask(lengths)
    copies[2].wait()
    for f in range(9):
        kept = jnp.where(in_range, raw[f].reshape(64, 1024), jnp.zeros((), BF16))
        masked[f * 64 : f * 64 + 64, :] = kept
    sent = []
    for block in range(4):
        sorted_rows = dot(chosen_ref[block * 256 : block * 256 + 256, :], masked[...], NT)
        part = slice(block * 128, block * 128 + 128)
        out[part] = sorted_rows.astype(BF16).reshape(128, 2, 576)
        copy = pltpu.make_async_copy(out.at[part], out_hbm.at[part], out_sems.at[block])
        copy.start()
        sent.append(copy)
    for copy in sent:
        copy.wait()
    kept_choice.wait()


def restore_kernel(length_ref, chosen_ref, data_ref, out_hbm, turned, out, sems):
    in_range = wave_mask(length_ref)
    for block in range(8):
        rows = data_ref[block * 64 : block * 64 + 64].reshape(128, 576)
        turned[:, block * 128 : block * 128 + 128] = rows.T
    sent = []
    for start, size in ((0, 4), (4, 4), (8, 1)):
        restored = dot(turned[start * 64 : (start + size) * 64, :], chosen_ref[...])
        for f in range(size):
            kept = jnp.where(in_range, restored[f * 64 : f * 64 + 64, :], 0.0).astype(BF16)
            out[start + f] = kept.reshape(32, 2, 1024)
        part = slice(start, start + size)
        copy = pltpu.make_async_copy(out.at[part], out_hbm.at[part], sems.at[len(sent)])
        copy.start()
        sent.append(copy)
    for copy in sent:
        copy.wait()


def order_pairs(row_length, wave_order, fourier):
    return pl.pallas_call(
        order_kernel,
        out_shape=(
            pltpu.HBM((512, 2, 576), BF16),
            pltpu.HBM((1024, 1024), BF16),
        ),
        in_specs=[HBM, HBM, HBM],
        out_specs=(HBM, HBM),
        scratch_shapes=[
            pltpu.VMEM((1, 32), jnp.int32),
            pltpu.VMEM((1, 512), jnp.int32),
            pltpu.VMEM((9, 32, 2, 1024), BF16),
            pltpu.VMEM((576, 1024), BF16),
            pltpu.VMEM((512, 2, 576), BF16),
            pltpu.VMEM((1024, 1024), BF16),
            pltpu.SemaphoreType.DMA((4,)),
            pltpu.SemaphoreType.DMA((4,)),
        ],
        compiler_params=pltpu.CompilerParams(vmem_limit_bytes=16 * 1024 * 1024),
    )(*(pltpu.with_memory_space_constraint(x, pltpu.HBM) for x in (row_length, wave_order, fourier)))


def restore_waves(row_length, chosen, data):
    return pl.pallas_call(
        restore_kernel,
        out_shape=jax.ShapeDtypeStruct((9, 32, 2, 1024), BF16),
        in_specs=[VMEM, VMEM, VMEM],
        out_specs=HBM,
        scratch_shapes=[
            pltpu.VMEM((576, 1024), BF16),
            pltpu.VMEM((9, 32, 2, 1024), BF16),
            pltpu.SemaphoreType.DMA((3,)),
        ],
        compiler_params=pltpu.CompilerParams(vmem_limit_bytes=16 * 1024 * 1024),
    )(row_length, chosen, data)


def exchange(chunks):
    return lax.all_to_all(chunks, ("band", "field"), split_axis=0, concat_axis=0, tiled=True)


def per_device(fourier, row_length, wave_order, legendre, vertical):
    position = lax.axis_index("band") * lax.axis_size("field") + lax.axis_index("field")
    lengths = row_length.reshape(1, 32)
    outgoing, chosen = order_pairs(lengths, wave_order.reshape(1, 512), fourier)
    arrived = exchange(outgoing)
    boundary = 1024 - lax.dynamic_slice_in_dim(wave_order, position, 1)
    result = transform_pair(boundary, arrived, vertical, *prepare(boundary, legendre[0]))
    return restore_waves(lengths, chosen, exchange(result))


def solution(mesh):
    placed = (P("field", "band", None, None), P("band"), P(), P(("band", "field"), None, None), P())
    return jax.shard_map(
        per_device,
        mesh=mesh,
        in_specs=placed,
        out_specs=P("field", "band", None, None),
        check_vma=False,
    )
```
